32 devices in a mesh: dp: 8 (over z, x), fsdp: 4 (over y, core).
Axes of the slice: x: 2, y: 2, z: 4, core: 2. Of those that a mesh axis runs over, the one named last changes fastest.
Arguments:
- block_input: bfloat16 [16384, 1024], P(('dp', 'fsdp')), may hold values from -6 to 6
- out_cotangent: bfloat16 [16384, 1024], P(('dp', 'fsdp')), may hold values from -6 to 6
- inproj: float32 [1024, 3072], P(None, ('dp', 'fsdp')), may hold values from -0.1875 to 0.1875
- convtaps: float32 [3, 1024], P(None, ('dp', 'fsdp')), may hold values from -3.5 to 3.5
- outproj: float32 [1024, 1024], P(None, ('dp', 'fsdp')), may hold values from -0.1875 to 0.1875
- gateproj: float32 [1024, 4608], P(None, ('dp', 'fsdp')), may hold values from -0.1875 to 0.1875
- upproj: float32 [1024, 4608], P(None, ('dp', 'fsdp')), may hold values from -0.1875 to 0.1875
- downproj: float32 [4608, 1024], P(None, ('dp', 'fsdp')), may hold values from -0.1875 to 0.1875
- normgains: float32 [2, 1024], P(None, ('dp', 'fsdp')), may hold values from 0.1 to 1.9
- first_inproj: float32 [1024, 3072], P(None, ('dp', 'fsdp')), may hold values from -128 to 128
- first_convtaps: float32 [3, 1024], P(None, ('dp', 'fsdp')), may hold values from -128 to 128
- first_outproj: float32 [1024, 1024], P(None, ('dp', 'fsdp')), may hold values from -128 to 128
- first_gateproj: float32 [1024, 4608], P(None, ('dp', 'fsdp')), may hold values from -40 to 40
- first_upproj: float32 [1024, 4608], P(None, ('dp', 'fsdp')), may hold values from -40 to 40
- first_downproj: float32 [4608, 1024], P(None, ('dp', 'fsdp')), may hold values from -40 to 40
- first_normgains: float32 [2, 1024], P(None, ('dp', 'fsdp')), may hold values from -160 to 160
- second_inproj: float32 [1024, 3072], P(None, ('dp', 'fsdp')), may hold values from 58.9824 to 235.9296
- second_convtaps: float32 [3, 1024], P(None, ('dp', 'fsdp')), may hold values from 58.9824 to 235.9296
- second_outproj: float32 [1024, 1024], P(None, ('dp', 'fsdp')), may hold values from 58.9824 to 235.9296
- second_gateproj: float32 [1024, 4608], P(None, ('dp', 'fsdp')), may hold values from 4.58752 to 18.35008
- second_upproj: float32 [1024, 4608], P(None, ('dp', 'fsdp')), may hold values from 4.9152 to 19.6608
- second_downproj: float32 [4608, 1024], P(None, ('dp', 'fsdp')), may hold values from 4.096 to 16.384
- second_normgains: float32 [2, 1024], P(None, ('dp', 'fsdp')), may hold values from 81.92 to 327.68
Outputs:
- block_output: bfloat16 [16384, 1024], P(('dp', 'fsdp'))
- input_grad: float32 [16384, 1024], P(('dp', 'fsdp'))
- moment_inproj: float32 [1024, 3072], P(None, ('dp', 'fsdp'))
- square_inproj: float32 [1024, 3072], P(None, ('dp', 'fsdp'))
- weight_inproj: float32 [1024, 3072], P(None, ('dp', 'fsdp'))
- moment_convtaps: float32 [3, 1024], P(None, ('dp', 'fsdp'))
- square_convtaps: float32 [3, 1024], P(None, ('dp', 'fsdp'))
- weight_convtaps: float32 [3, 1024], P(None, ('dp', 'fsdp'))
- moment_outproj: float32 [1024, 1024], P(None, ('dp', 'fsdp'))
- square_outproj: float32 [1024, 1024], P(None, ('dp', 'fsdp'))
- weight_outproj: float32 [1024, 1024], P(None, ('dp', 'fsdp'))
- moment_gateproj: float32 [1024, 4608], P(None, ('dp', 'fsdp'))
- square_gateproj: float32 [1024, 4608], P(None, ('dp', 'fsdp'))
- weight_gateproj: float32 [1024, 4608], P(None, ('dp', 'fsdp'))
- moment_upproj: float32 [1024, 4608], P(None, ('dp', 'fsdp'))
- square_upproj: float32 [1024, 4608], P(None, ('dp', 'fsdp'))
- weight_upproj: float32 [1024, 4608], P(None, ('dp', 'fsdp'))
- moment_downproj: float32 [4608, 1024], P(None, ('dp', 'fsdp'))
- square_downproj: float32 [4608, 1024], P(None, ('dp', 'fsdp'))
- weight_downproj: float32 [4608, 1024], P(None, ('dp', 'fsdp'))
- moment_normgains: float32 [2, 1024], P(None, ('dp', 'fsdp'))
- square_normgains: float32 [2, 1024], P(None, ('dp', 'fsdp'))
- weight_normgains: float32 [2, 1024], P(None, ('dp', 'fsdp'))
The draws below stay inside these ranges and needn't reach their ends.
All inputs are finite; a program needn't handle non-finite values.
Results may differ from the reference program's by a relative error of at most 0.012.
The reference program's roundings to bfloat16 on the way count: a program that leaves them out, or rounds other values in their place, can miss the bound.
Values may be sent and summed in bfloat16 or wider, within the bound.
A program may use at most 384 MiB of HBM per device.

```python
import math
import jax
import jax.numpy as jnp
from jax import lax

D = 1024
FF = 4608
KERNEL = 3
SEQ = 512
STEP = 10
TOKENS = 16384


def strengthened(drawn, key, source, target, shards_of, factor):
    owner, partner = [(jnp.arange(drawn.shape[dim]) // (drawn.shape[dim] // shards_of)).reshape([-1 if axis == dim else 1 for axis in range(drawn.ndim)]) for dim in (source, target)]
    chosen = jax.random.permutation(key, shards_of)[partner]
    strong = (owner == chosen) | (owner == (partner + shards_of // 2) % shards_of)
    return jnp.where(strong, factor * drawn, drawn)


def shard_levels(rng, dims, pieces, least, largest):
    def one(dim, parts):
        heights = jax.random.uniform(jax.random.fold_in(jax.random.fold_in(rng, 6), dim), (parts,), jnp.float32, least / len(pieces), largest / len(pieces))
        return jnp.repeat(jnp.exp(heights), dims[dim] // parts).reshape((-1,) + (1,) * (len(dims) - dim - 1))

    factor_of = one(*pieces[0])
    for cut in pieces[1:]:
        factor_of = factor_of * one(*cut)
    return factor_of


def centred(key, extent, deviation, limit, pieces=(), dtype=jnp.bfloat16):
    entries = jax.random.normal(key, extent, jnp.float32) * deviation
    if len(pieces) > 0:
        entries = shard_levels(key, extent, pieces, -0.22, 0.18) * entries
    return jnp.clip(entries, min=-limit, max=limit).astype(dtype)


def bell_draw_with(rng, extent, scale, reach, pieces, heavy, kind=jnp.bfloat16):
    values = scale * jax.random.normal(rng, extent, jnp.float32)
    if pieces:
        values = values * shard_levels(rng, extent, pieces, -0.22, 0.18)
    return jnp.clip(strengthened(values, jax.random.fold_in(rng, 3), *heavy), -reach, reach).astype(kind)


def setup_inputs(seed: int = 0) -> dict:
    keys = jax.random.split(jax.random.key(seed), 24)
    return {
        "block_input": centred(keys[0], (TOKENS, D), 1.0, 6.0, ((0, 32),)),
        "out_cotangent": bell_draw_with(keys[1], (TOKENS, D), 1.0, 6.0, ((0, 32),), (0, 1, 32, 2.75)),
        "inproj": centred(keys[2], (D, 3 * D), D ** -0.5, 0.1875, ((1, 32),), jnp.float32),
        "convtaps": centred(keys[3], (KERNEL, D), KERNEL ** -0.5, 3.5, ((1, 32),), jnp.float32),
        "outproj": centred(keys[4], (D, D), D ** -0.5, 0.1875, ((1, 32),), jnp.float32),
        "gateproj": centred(keys[5], (D, FF), D ** -0.5, 0.1875, ((1, 32),), jnp.float32),
        "upproj": centred(keys[6], (D, FF), D ** -0.5, 0.1875, ((1, 32),), jnp.float32),
        "downproj": centred(keys[7], (FF, D), (FF // 4) ** -0.5, 0.1875, ((1, 32),), jnp.float32),
        "normgains": jnp.clip(1.0 + 0.18 * jax.random.normal(keys[8], (2, D), jnp.float32), 0.1, 1.9),
        "first_inproj": centred(keys[9], (D, 3 * D), (0.1 * (3.6 * TOKENS) ** 0.5), 128.0, ((1, 32),), jnp.float32),
        "first_convtaps": centred(keys[10], (KERNEL, D), (0.1 * (3.6 * TOKENS) ** 0.5), 128.0, ((1, 32),), jnp.float32),
        "first_outproj": centred(keys[11], (D, D), (0.1 * (3.6 * TOKENS) ** 0.5), 128.0, ((1, 32),), jnp.float32),
        "first_gateproj": centred(keys[12], (D, FF), (0.1 * (0.28 * TOKENS) ** 0.5), 40.0, ((1, 32),), jnp.float32),
        "first_upproj": centred(keys[13], (D, FF), (0.1 * (0.3 * TOKENS) ** 0.5), 40.0, ((1, 32),), jnp.float32),
        "first_downproj": centred(keys[14], (FF, D), (0.1 * (0.25 * TOKENS) ** 0.5), 40.0, ((1, 32),), jnp.float32),
        "first_normgains": centred(keys[15], (2, D), (0.1 * (5.0 * TOKENS) ** 0.5), 160.0, ((1, 32),), jnp.float32),
        "second_inproj": jnp.clip(jnp.exp(math.log(235.9296) - 1.3862944 * jax.random.uniform(keys[16], (D, 3 * D), jnp.float32) ** shard_levels(keys[16], (D, 3 * D), ((1, 32),), -0.2, 0.2)), 58.9824, 235.9296),
        "second_convtaps": jnp.clip(jnp.exp(math.log(235.9296) - 1.3862944 * jax.random.uniform(keys[17], (KERNEL, D), jnp.float32) ** shard_levels(keys[17], (KERNEL, D), ((1, 32),), -0.2, 0.2)), 58.9824, 235.9296),
        "second_outproj": jnp.clip(jnp.exp(math.log(235.9296) - 1.3862944 * jax.random.uniform(keys[18], (D, D), jnp.float32) ** shard_levels(keys[18], (D, D), ((1, 32),), -0.2, 0.2)), 58.9824, 235.9296),
        "second_gateproj": jnp.clip(jnp.exp(math.log(18.35008) - 1.3862944 * jax.random.uniform(keys[19], (D, FF), jnp.float32) ** shard_levels(keys[19], (D, FF), ((1, 32),), -0.2, 0.2)), 4.58752, 18.35008),
        "second_upproj": jnp.clip(jnp.exp(math.log(19.6608) - 1.3862944 * jax.random.uniform(keys[20], (D, FF), jnp.float32) ** shard_levels(keys[20], (D, FF), ((1, 32),), -0.2, 0.2)), 4.9152, 19.6608),
        "second_downproj": jnp.clip(jnp.exp(math.log(16.384) - 1.3862944 * jax.random.uniform(keys[21], (FF, D), jnp.float32) ** shard_levels(keys[21], (FF, D), ((1, 32),), -0.2, 0.2)), 4.096, 16.384),
        "second_normgains": jnp.clip(jnp.exp(math.log(327.68) - 1.3862944 * jax.random.uniform(keys[22], (2, D), jnp.float32) ** shard_levels(keys[22], (2, D), ((1, 32),), -0.2, 0.2)), 81.92, 327.68),
    }


@jax.custom_vjp
def low(v):
    return lax.optimization_barrier(v.astype(jnp.bfloat16)).astype(jnp.float32)

@jax.custom_vjp
def low_back(v):
    return v

def low_keep(v):
    return (low(v), None)

def low_pass(kept, grad):
    return (grad,)

def back_keep(v):
    return (v, None)

def back_low(kept, grad):
    return (low(grad),)
low.defvjp(low_keep, low_pass)
low_back.defvjp(back_keep, back_low)
eps_norm = 1e-05
beta_one = 0.9
beta_two = 0.999
eps_adam = 1e-08
rates = (0.06, 0.5, 0.06, 0.06, 0.06, 0.06, 0.5)
decays = (0.01, 0.01, 0.01, 0.01, 0.01, 0.01, 0.0)

def matmul(left, right):
    return jnp.dot(left, right, precision=lax.Precision.HIGHEST, preferred_element_type=jnp.float32)

def norm_rows(values, gain):
    return values * lax.rsqrt(lax.optimization_barrier(jnp.mean(values * values, axis=-1, keepdims=True)) + eps_norm) * gain

def mix_conv(projected, filters):
    width = filters.shape[1]
    seqcount = projected.shape[0] // SEQ
    gated = projected[:, :width] * projected[:, 2 * width:]
    blocks = gated.reshape(seqcount, SEQ, width)
    padded = jnp.pad(blocks, ((0, 0), (KERNEL - 1, 0), (0, 0)))
    mixed = filters[0] * padded[:, 0:SEQ]
    for offset in range(1, KERNEL):
        mixed = mixed + filters[offset] * padded[:, offset:offset + SEQ]
    return projected[:, width:2 * width] * mixed.reshape(-1, width)

def block_forward(weights, resid):
    in_weight, filters, out_weight, gate_weight, up_weight, down_weight, gains = [low(item) for item in weights]
    normed = low(norm_rows(resid, gains[0]))
    projected = low_back(matmul(normed, in_weight))
    mixed = low(mix_conv(projected, filters))
    branch = low_back(matmul(mixed, out_weight))
    middle = resid + branch
    normed_two = low(norm_rows(middle, gains[1]))
    gate = low_back(matmul(normed_two, gate_weight))
    upward = low_back(matmul(normed_two, up_weight))
    hidden = low(jax.nn.silu(gate) * upward)
    ffn_out = low_back(matmul(hidden, down_weight))
    return middle + ffn_out

def adamw_step(param, grad, first, second, rate, decay):
    moment = beta_one * first + (1.0 - beta_one) * grad
    square = beta_two * second + (1.0 - beta_two) * grad * grad
    mhat = moment / (1.0 - beta_one ** STEP)
    vhat = square / (1.0 - beta_two ** STEP)
    updated = param - rate * (mhat / (jnp.sqrt(vhat) + eps_adam) + decay * param)
    return (moment, square, updated)

def reference(block_input, out_cotangent, inproj, convtaps, outproj, gateproj, upproj, downproj, normgains, first_inproj, first_convtaps, first_outproj, first_gateproj, first_upproj, first_downproj, first_normgains, second_inproj, second_convtaps, second_outproj, second_gateproj, second_upproj, second_downproj, second_normgains):
    weights = (inproj, convtaps, outproj, gateproj, upproj, downproj, normgains)
    firsts = (first_inproj, first_convtaps, first_outproj, first_gateproj, first_upproj, first_downproj, first_normgains)
    seconds = (second_inproj, second_convtaps, second_outproj, second_gateproj, second_upproj, second_downproj, second_normgains)
    seqcount = block_input.shape[0] // SEQ
    group = math.gcd(seqcount, max(1, 4096 // SEQ))
    count = seqcount // group
    inputs = block_input.astype(jnp.float32).reshape(count, group * SEQ, D)
    cotans = out_cotangent.astype(jnp.float32).reshape(count, group * SEQ, D)

    def group_step(totals, pair):
        resid, cotan = pair
        result, backward = jax.vjp(block_forward, weights, resid)
        wgrads, xgrad = backward(cotan)
        totals = tuple((total + wgrad for total, wgrad in zip(totals, wgrads)))
        return (totals, (result.astype(jnp.bfloat16), xgrad))
    initial = tuple((jnp.zeros(item.shape, jnp.float32) for item in weights))
    totals, (results, xgrads) = lax.scan(group_step, initial, (inputs, cotans))
    outputs = [results.reshape(-1, D), xgrads.reshape(-1, D)]
    for position in range(7):
        moment, square, updated = adamw_step(weights[position], totals[position], firsts[position], seconds[position], rates[position], decays[position])
        outputs = outputs + [moment, square, updated]
    return tuple(outputs)
```

```python
import jax
import jax.numpy as jnp
from jax import lax
from jax.sharding import PartitionSpec as P

KERNEL = 3
SEQ = 512
STEP = 10


eps_norm = 1e-05
beta_one = 0.9
beta_two = 0.999
eps_adam = 1e-08
rates = (0.06, 0.5, 0.06, 0.06, 0.06, 0.06, 0.5)
decays = (0.01, 0.01, 0.01, 0.01, 0.01, 0.01, 0.0)


def norm_rows(values, gain):
    return values * lax.rsqrt(jnp.mean(values * values, axis=-1, keepdims=True) + eps_norm) * gain


def mix_conv(projected, filters):
    width = filters.shape[1]
    seqcount = projected.shape[0] // SEQ
    gated = projected[:, :width] * projected[:, 2 * width :]
    blocks = gated.reshape(seqcount, SEQ, width)
    padded = jnp.pad(blocks, ((0, 0), (KERNEL - 1, 0), (0, 0)))
    mixed = filters[0] * padded[:, 0:SEQ]
    for offset in range(1, KERNEL):
        mixed = mixed + filters[offset] * padded[:, offset : offset + SEQ]
    return projected[:, width : 2 * width] * mixed.reshape(-1, width)


def swiglu(gate, upward):
    return jax.nn.silu(gate) * upward


def adamw_step(param, grad, first, second, rate, decay):
    moment = beta_one * first + (1.0 - beta_one) * grad
    square = beta_two * second + (1.0 - beta_two) * grad * grad
    mhat = moment / (1.0 - beta_one**STEP)
    vhat = square / (1.0 - beta_two**STEP)
    updated = param - rate * (mhat / (jnp.sqrt(vhat) + eps_adam) + decay * param)
    return (moment, square, updated)


def shards(
    block_input,
    out_cotangent,
    inproj,
    convtaps,
    outproj,
    gateproj,
    upproj,
    downproj,
    normgains,
    first_inproj,
    first_convtaps,
    first_outproj,
    first_gateproj,
    first_upproj,
    first_downproj,
    first_normgains,
    second_inproj,
    second_convtaps,
    second_outproj,
    second_gateproj,
    second_upproj,
    second_downproj,
    second_normgains,
):
    masters = (inproj, convtaps, outproj, gateproj, upproj, downproj, normgains)
    firsts = (
        first_inproj,
        first_convtaps,
        first_outproj,
        first_gateproj,
        first_upproj,
        first_downproj,
        first_normgains,
    )
    seconds = (
        second_inproj,
        second_convtaps,
        second_outproj,
        second_gateproj,
        second_upproj,
        second_downproj,
        second_normgains,
    )
    shard_axes = ("dp", "fsdp")
    in_weight, out_weight, gate_weight, up_weight, down_weight = (
        lax.all_gather(item.astype(jnp.bfloat16).T, shard_axes, axis=0, tiled=True)
        for item in (inproj, outproj, gateproj, upproj, downproj)
    )
    small = jnp.concatenate([convtaps, normgains], axis=0).astype(jnp.bfloat16)
    small = lax.all_gather(small, shard_axes, axis=1, tiled=True).astype(jnp.float32)
    filters = small[:KERNEL]
    gain_one = small[KERNEL]
    gain_two = small[KERNEL + 1]
    resid = block_input.astype(jnp.float32)
    normed = norm_rows(resid, gain_one).astype(jnp.bfloat16)
    projected = jnp.einsum("td,ed->te", normed, in_weight, preferred_element_type=jnp.float32)
    mixed = mix_conv(projected, filters).astype(jnp.bfloat16)
    middle = resid + jnp.einsum("td,ed->te", mixed, out_weight, preferred_element_type=jnp.float32)
    normed_two = norm_rows(middle, gain_two).astype(jnp.bfloat16)
    gate = jnp.einsum("td,fd->tf", normed_two, gate_weight, preferred_element_type=jnp.float32)
    upward = jnp.einsum("td,fd->tf", normed_two, up_weight, preferred_element_type=jnp.float32)
    hidden = swiglu(gate, upward).astype(jnp.bfloat16)
    ffn_out = jnp.einsum("tf,df->td", hidden, down_weight, preferred_element_type=jnp.float32)
    block_output = (middle + ffn_out).astype(jnp.bfloat16)
    cotan = out_cotangent.astype(jnp.float32)

    def owned_sum(left, right):
        part = jnp.einsum("te,td->ed", left, right, preferred_element_type=jnp.float32)
        part = part.astype(jnp.bfloat16)
        total = lax.psum_scatter(part, shard_axes, scatter_dimension=0, tiled=True)
        return total.astype(jnp.float32).T

    grad_down = owned_sum(out_cotangent, hidden)
    d_hidden = jnp.einsum(
        "td,df->tf", out_cotangent, down_weight, preferred_element_type=jnp.float32
    )
    unused_value, swiglu_back = jax.vjp(swiglu, gate, upward)
    d_gate, d_upward = swiglu_back(d_hidden)
    d_gate = d_gate.astype(jnp.bfloat16)
    d_upward = d_upward.astype(jnp.bfloat16)
    grad_gate = owned_sum(d_gate, normed_two)
    grad_up = owned_sum(d_upward, normed_two)
    d_normed_two = jnp.einsum(
        "tf,fd->td", d_gate, gate_weight, preferred_element_type=jnp.float32
    ) + jnp.einsum("tf,fd->td", d_upward, up_weight, preferred_element_type=jnp.float32)
    unused_two, norm_back_two = jax.vjp(norm_rows, middle, gain_two)
    d_middle_norm, grad_gain_two = norm_back_two(d_normed_two)
    d_middle = cotan + d_middle_norm
    d_branch = d_middle.astype(jnp.bfloat16)
    grad_out = owned_sum(d_branch, mixed)
    d_mixed = jnp.einsum("te,ed->td", d_branch, out_weight, preferred_element_type=jnp.float32)
    unused_three, conv_back = jax.vjp(mix_conv, projected, filters)
    d_projected, grad_filters = conv_back(d_mixed)
    d_projected = d_projected.astype(jnp.bfloat16)
    grad_in = owned_sum(d_projected, normed)
    d_normed = jnp.einsum("te,ed->td", d_projected, in_weight, preferred_element_type=jnp.float32)
    unused_four, norm_back_one = jax.vjp(norm_rows, resid, gain_one)
    d_resid_norm, grad_gain_one = norm_back_one(d_normed)
    input_grad = d_middle + d_resid_norm
    grad_small = jnp.concatenate([grad_filters, grad_gain_one[None], grad_gain_two[None]], axis=0)
    grad_small = lax.psum(grad_small, shard_axes)
    share = convtaps.shape[1]
    grad_small = lax.dynamic_slice_in_dim(
        grad_small, lax.axis_index(shard_axes) * share, share, axis=1
    )
    owned = (
        grad_in,
        grad_small[:KERNEL],
        grad_out,
        grad_gate,
        grad_up,
        grad_down,
        grad_small[KERNEL:],
    )
    outputs = [block_output, input_grad]
    for position in range(7):
        moment, square, updated = adamw_step(
            masters[position],
            owned[position],
            firsts[position],
            seconds[position],
            rates[position],
            decays[position],
        )
        outputs = outputs + [moment, square, updated]
    return tuple(outputs)


def solution(mesh):
    return jax.shard_map(
        shards,
        mesh=mesh,
        in_specs=(
            P(("dp", "fsdp"), None),
            P(("dp", "fsdp"), None),
            P(None, ("dp", "fsdp")),
            P(None, ("dp", "fsdp")),
            P(None, ("dp", "fsdp")),
            P(None, ("dp", "fsdp")),
            P(None, ("dp", "fsdp")),
            P(None, ("dp", "fsdp")),
            P(None, ("dp", "fsdp")),
            P(None, ("dp", "fsdp")),
            P(None, ("dp", "fsdp")),
            P(None, ("dp", "fsdp")),
            P(None, ("dp", "fsdp")),
            P(None, ("dp", "fsdp")),
            P(None, ("dp", "fsdp")),
            P(None, ("dp", "fsdp")),
            P(None, ("dp", "fsdp")),
            P(None, ("dp", "fsdp")),
            P(None, ("dp", "fsdp")),
            P(None, ("dp", "fsdp")),
            P(None, ("dp", "fsdp")),
            P(None, ("dp", "fsdp")),
            P(None, ("dp", "fsdp")),
        ),
        out_specs=(
            P(("dp", "fsdp"), None),
            P(("dp", "fsdp"), None),
            P(None, ("dp", "fsdp")),
            P(None, ("dp", "fsdp")),
            P(None, ("dp", "fsdp")),
            P(None, ("dp", "fsdp")),
            P(None, ("dp", "fsdp")),
            P(None, ("dp", "fsdp")),
            P(None, ("dp", "fsdp")),
            P(None, ("dp", "fsdp")),
            P(None, ("dp", "fsdp")),
            P(None, ("dp", "fsdp")),
            P(None, ("dp", "fsdp")),
            P(None, ("dp", "fsdp")),
            P(None, ("dp", "fsdp")),
            P(None, ("dp", "fsdp")),
            P(None, ("dp", "fsdp")),
            P(None, ("dp", "fsdp")),
            P(None, ("dp", "fsdp")),
            P(None, ("dp", "fsdp")),
            P(None, ("dp", "fsdp")),
            P(None, ("dp", "fsdp")),
            P(None, ("dp", "fsdp")),
        ),
        check_vma=False,
    )
```

```python
import jax
import jax.numpy as jnp
from jax import lax
from jax.sharding import PartitionSpec as P

KERNEL = 3
SEQ = 512
STEP = 10


eps_norm = 1e-05
beta_one = 0.9
beta_two = 0.999
eps_adam = 1e-08
rates = (0.06, 0.5, 0.06, 0.06, 0.06, 0.06, 0.5)
decays = (0.01, 0.01, 0.01, 0.01, 0.01, 0.01, 0.0)


def norm_rows(values, gain):
    return values * lax.rsqrt(jnp.mean(values * values, axis=-1, keepdims=True) + eps_norm) * gain


def mix_conv(projected, filters):
    width = filters.shape[1]
    seqcount = projected.shape[0] // SEQ
    gated = projected[:, :width] * projected[:, 2 * width :]
    blocks = gated.reshape(seqcount, SEQ, width)
    padded = jnp.pad(blocks, ((0, 0), (KERNEL - 1, 0), (0, 0)))
    mixed = filters[0] * padded[:, 0:SEQ]
    for offset in range(1, KERNEL):
        mixed = mixed + filters[offset] * padded[:, offset : offset + SEQ]
    return projected[:, width : 2 * width] * mixed.reshape(-1, width)


def swiglu(gate, upward):
    return jax.nn.silu(gate) * upward


def adamw_step(param, grad, first, second, rate, decay):
    moment = beta_one * first + (1.0 - beta_one) * grad
    square = beta_two * second + (1.0 - beta_two) * grad * grad
    mhat = moment / (1.0 - beta_one**STEP)
    vhat = square / (1.0 - beta_two**STEP)
    updated = param - rate * (mhat / (jnp.sqrt(vhat) + eps_adam) + decay * param)
    return (moment, square, updated)


AXES = ("dp", "fsdp")
CORES = 2


def grid_shape():
    rows = lax.axis_size("fsdp") // CORES
    return {"z": lax.axis_size("dp") // rows, "x": rows, "y": rows, "c": CORES}


def position(dim):
    sizes = grid_shape()
    index = lax.axis_index(AXES)
    below = {"z": ("x", "y", "c"), "x": ("y", "c"), "y": ("c",), "c": ()}[dim]
    for lower in below:
        index = index // sizes[lower]
    return index % sizes[dim]


def shift_pairs(dim, step, allowed):
    sizes = grid_shape()
    stride = {
        "z": sizes["x"] * sizes["y"] * sizes["c"],
        "x": sizes["y"] * sizes["c"],
        "y": sizes["c"],
        "c": 1,
    }[dim]
    total = sizes["z"] * sizes["x"] * sizes["y"] * sizes["c"]
    pairs = []
    for device in range(total):
        place = device // stride % sizes[dim]
        if allowed(place) and 0 <= place + step < sizes[dim]:
            pairs.append((device, device + step * stride))
    return pairs


def swap(value, dim):
    pairs = shift_pairs(dim, 1, lambda place: True) + shift_pairs(dim, -1, lambda place: True)
    return lax.ppermute(value, AXES, pairs)


def line_gather(value, dim):
    size = grid_shape()[dim]
    place = position(dim)
    if size == 2:
        other = swap(value, dim)
        first = place == 0
        return jnp.stack([jnp.where(first, value, other), jnp.where(first, other, value)])
    from_low = []
    from_high = []
    low = value
    high = value
    for step in range(1, size):
        low = lax.ppermute(low, AXES, shift_pairs(dim, 1, lambda p: p >= step - 1))
        high = lax.ppermute(high, AXES, shift_pairs(dim, -1, lambda p: p <= size - step))
        from_low.append(low)
        from_high.append(high)
    every = jnp.stack(from_low[::-1] + [value] + from_high)
    return lax.dynamic_slice_in_dim(every, size - 1 - place, size, axis=0)


def mesh_gather(value, order):
    shape = value.shape
    for dim in order:
        value = line_gather(value, dim)
    names = order[::-1]
    value = value.transpose([names.index(dim) for dim in "zxyc"] + [4, 5])
    return value.reshape((-1,) + shape)


def pick(parts, axis, index):
    size = parts.shape[axis]
    return lax.dynamic_index_in_dim(parts, jnp.clip(index, 0, size - 1), axis, keepdims=False)


def add_low(left, right):
    return (left.astype(jnp.float32) + right.astype(jnp.float32)).astype(jnp.bfloat16)


def line_sum(parts, axis, dim, last):
    size = grid_shape()[dim]
    place = position(dim)
    own = pick(parts, axis, place)
    if size == 2:
        arrived = swap(pick(parts, axis, 1 - place), dim).astype(jnp.float32)
    else:
        up = None
        down = None
        for step in range(1, size):
            send_up = pick(parts, axis, place + size - step)
            send_down = pick(parts, axis, place - size + step)
            if step > 1:
                send_up = add_low(send_up, up)
                send_down = add_low(send_down, down)
            up = lax.ppermute(send_up, AXES, shift_pairs(dim, 1, lambda p: p <= step - 1))
            down = lax.ppermute(send_down, AXES, shift_pairs(dim, -1, lambda p: p >= size - step))
        arrived = up.astype(jnp.float32) + down.astype(jnp.float32)
    total = own.astype(jnp.float32) + arrived
    return total if last else total.astype(jnp.bfloat16)


def mesh_sum(parts, order):
    sizes = grid_shape()
    parts = parts.reshape(tuple(sizes[dim] for dim in "zxyc") + parts.shape[1:])
    names = ["z", "x", "y", "c"]
    for dim in order:
        axis = names.index(dim)
        names.pop(axis)
        parts = line_sum(parts, axis, dim, len(names) == 0)
    return parts


def shards(
    block_input,
    out_cotangent,
    inproj,
    convtaps,
    outproj,
    gateproj,
    upproj,
    downproj,
    normgains,
    first_inproj,
    first_convtaps,
    first_outproj,
    first_gateproj,
    first_upproj,
    first_downproj,
    first_normgains,
    second_inproj,
    second_convtaps,
    second_outproj,
    second_gateproj,
    second_upproj,
    second_downproj,
    second_normgains,
):
    masters = (inproj, convtaps, outproj, gateproj, upproj, downproj, normgains)
    firsts = (
        first_inproj,
        first_convtaps,
        first_outproj,
        first_gateproj,
        first_upproj,
        first_downproj,
        first_normgains,
    )
    seconds = (
        second_inproj,
        second_convtaps,
        second_outproj,
        second_gateproj,
        second_upproj,
        second_downproj,
        second_normgains,
    )
    owners = lax.axis_size(AXES)
    width = block_input.shape[1]
    share = convtaps.shape[1]
    low = [
        item.astype(jnp.bfloat16).T for item in (inproj, outproj, gateproj, upproj, downproj)
    ]
    small = jnp.concatenate([convtaps, normgains], axis=0).astype(jnp.bfloat16)
    small = jnp.pad(small, ((0, 8 - KERNEL - 2), (0, width - share)))
    rows_in, rows_out = low[0].shape[0], low[1].shape[0]
    first = mesh_gather(jnp.concatenate([low[0], small]), "xyzc")
    second = mesh_gather(jnp.concatenate([low[2], low[1]]), "yzxc")
    up_weight = mesh_gather(low[3], "zxyc").reshape(-1, width)
    down_weight = mesh_gather(low[4], "zxyc").reshape(width, -1)
    in_weight = first[:, :rows_in].reshape(-1, width)
    small = first[:, rows_in : rows_in + KERNEL + 2, :share]
    small = small.transpose(1, 0, 2).reshape(KERNEL + 2, -1).astype(jnp.float32)
    gate_weight = second[:, :-rows_out].reshape(-1, width)
    out_weight = second[:, -rows_out:].reshape(-1, width)
    filters = small[:KERNEL]
    gain_one = small[KERNEL]
    gain_two = small[KERNEL + 1]
    resid = block_input.astype(jnp.float32)
    normed = norm_rows(resid, gain_one).astype(jnp.bfloat16)
    projected = jnp.einsum("td,ed->te", normed, in_weight, preferred_element_type=jnp.float32)
    mixed = mix_conv(projected, filters).astype(jnp.bfloat16)
    middle = resid + jnp.einsum("td,ed->te", mixed, out_weight, preferred_element_type=jnp.float32)
    normed_two = norm_rows(middle, gain_two).astype(jnp.bfloat16)
    gate = jnp.einsum("td,fd->tf", normed_two, gate_weight, preferred_element_type=jnp.float32)
    upward = jnp.einsum("td,fd->tf", normed_two, up_weight, preferred_element_type=jnp.float32)
    hidden = swiglu(gate, upward).astype(jnp.bfloat16)
    ffn_out = jnp.einsum("tf,df->td", hidden, down_weight, preferred_element_type=jnp.float32)
    block_output = (middle + ffn_out).astype(jnp.bfloat16)
    cotan = out_cotangent.astype(jnp.float32)

    def gradient(left, right):
        part = jnp.einsum("te,td->ed", left, right, preferred_element_type=jnp.float32)
        part = part.astype(jnp.bfloat16)
        return part.reshape(owners, -1, part.shape[1])

    grad_down = mesh_sum(gradient(out_cotangent, hidden), "cyxz").T
    d_hidden = jnp.einsum(
        "td,df->tf", out_cotangent, down_weight, preferred_element_type=jnp.float32
    )
    unused_value, swiglu_back = jax.vjp(swiglu, gate, upward)
    d_gate, d_upward = swiglu_back(d_hidden)
    d_gate = d_gate.astype(jnp.bfloat16)
    d_upward = d_upward.astype(jnp.bfloat16)
    grad_gate = mesh_sum(gradient(d_gate, normed_two), "cxzy").T
    grad_up = mesh_sum(gradient(d_upward, normed_two), "cyxz").T
    d_normed_two = jnp.einsum(
        "tf,fd->td", d_gate, gate_weight, preferred_element_type=jnp.float32
    ) + jnp.einsum("tf,fd->td", d_upward, up_weight, preferred_element_type=jnp.float32)
    unused_two, norm_back_two = jax.vjp(norm_rows, middle, gain_two)
    d_middle_norm, grad_gain_two = norm_back_two(d_normed_two)
    d_middle = cotan + d_middle_norm
    d_branch = d_middle.astype(jnp.bfloat16)
    grad_out = mesh_sum(gradient(d_branch, mixed), "cxzy").T
    d_mixed = jnp.einsum("te,ed->td", d_branch, out_weight, preferred_element_type=jnp.float32)
    unused_three, conv_back = jax.vjp(mix_conv, projected, filters)
    d_projected, grad_filters = conv_back(d_mixed)
    d_projected = d_projected.astype(jnp.bfloat16)
    d_normed = jnp.einsum("te,ed->td", d_projected, in_weight, preferred_element_type=jnp.float32)
    unused_four, norm_back_one = jax.vjp(norm_rows, resid, gain_one)
    d_resid_norm, grad_gain_one = norm_back_one(d_normed)
    input_grad = d_middle + d_resid_norm
    grad_small = jnp.concatenate([grad_filters, grad_gain_one[None], grad_gain_two[None]], axis=0)
    grad_small = grad_small.astype(jnp.bfloat16).reshape(KERNEL + 2, owners, share)
    grad_small = jnp.pad(
        grad_small.transpose(1, 0, 2), ((0, 0), (0, 8 - KERNEL - 2), (0, width - share))
    )
    grad_first = jnp.concatenate([gradient(d_projected, normed), grad_small], axis=1)
    grad_first = mesh_sum(grad_first, "czyx")
    grad_in = grad_first[:rows_in].T
    grad_small = grad_first[rows_in : rows_in + KERNEL + 2, :share]
    owned = (
        grad_in,
        grad_small[:KERNEL],
        grad_out,
        grad_gate,
        grad_up,
        grad_down,
        grad_small[KERNEL:],
    )
    outputs = [block_output, input_grad]
    for position in range(7):
        moment, square, updated = adamw_step(
            masters[position],
            owned[position],
            firsts[position],
            seconds[position],
            rates[position],
            decays[position],
        )
        outputs = outputs + [moment, square, updated]
    return tuple(outputs)


def solution(mesh):
    return jax.shard_map(
        shards,
        mesh=mesh,
        in_specs=(
            P(("dp", "fsdp"), None),
            P(("dp", "fsdp"), None),
            P(None, ("dp", "fsdp")),
            P(None, ("dp", "fsdp")),
            P(None, ("dp", "fsdp")),
            P(None, ("dp", "fsdp")),
            P(None, ("dp", "fsdp")),
            P(None, ("dp", "fsdp")),
            P(None, ("dp", "fsdp")),
            P(None, ("dp", "fsdp")),
            P(None, ("dp", "fsdp")),
            P(None, ("dp", "fsdp")),
            P(None, ("dp", "fsdp")),
            P(None, ("dp", "fsdp")),
            P(None, ("dp", "fsdp")),
            P(None, ("dp", "fsdp")),
            P(None, ("dp", "fsdp")),
            P(None, ("dp", "fsdp")),
            P(None, ("dp", "fsdp")),
            P(None, ("dp", "fsdp")),
            P(None, ("dp", "fsdp")),
            P(None, ("dp", "fsdp")),
            P(None, ("dp", "fsdp")),
        ),
        out_specs=(
            P(("dp", "fsdp"), None),
            P(("dp", "fsdp"), None),
            P(None, ("dp", "fsdp")),
            P(None, ("dp", "fsdp")),
            P(None, ("dp", "fsdp")),
            P(None, ("dp", "fsdp")),
            P(None, ("dp", "fsdp")),
            P(None, ("dp", "fsdp")),
            P(None, ("dp", "fsdp")),
            P(None, ("dp", "fsdp")),
            P(None, ("dp", "fsdp")),
            P(None, ("dp", "fsdp")),
            P(None, ("dp", "fsdp")),
            P(None, ("dp", "fsdp")),
            P(None, ("dp", "fsdp")),
            P(None, ("dp", "fsdp")),
            P(None, ("dp", "fsdp")),
            P(None, ("dp", "fsdp")),
            P(None, ("dp", "fsdp")),
            P(None, ("dp", "fsdp")),
            P(None, ("dp", "fsdp")),
            P(None, ("dp", "fsdp")),
            P(None, ("dp", "fsdp")),
        ),
        check_vma=False,
    )
```
